128 devices in a mesh: group: 16 (over z, y), tp: 8 (over x, core).
Axes of the slice: x: 4, y: 4, z: 4, core: 2. Of those that a mesh axis runs over, the one named last changes fastest.
Arguments:
- fresh: bfloat16 [1536, 8, 64, 256], P(('group', 'tp')), may hold values from -18 to 18
- lengths: int32 [256], P('group'), may hold values from 1 to 508, as said below
- owner_table: int32 [256, 8], P('group'), may hold values from 0 to 95, as said below
- decode_slot: int32 [256], P('group'), may hold values from 0 to 255, as said below
- decode_table: int32 [256, 8], P('group'), may hold values from 0 to 127, as said below
- queries: bfloat16 [256, 4, 8192], P('group', None, 'tp'), may hold values from -24 to 24
- new_kv: bfloat16 [256, 4, 2048], P('group', None, 'tp'), may hold values from -6 to 6
Outputs:
- page_pool: bfloat16 [2048, 8, 64, 256], P('group', 'tp')
- attended: bfloat16 [256, 4, 8192], P('group', None, 'tp')
The draws below stay inside these ranges and needn't reach their ends.
Inputs may be any that keep to these rules, and one draw needn't show every extreme that they name: Each request has 1 to 8 pages, ceil(lengths[r] / 64); the pages of one group's requests add up to exactly 96; the pages of one home group's requests that are decoded on one group add up to at most 14, exactly 14 for some group; lengths[r] + 4 <= 512. `owner_table`: for j < ceil(lengths[r] / 64) the entries name distinct fresh pages across all requests of one home group; later entries are unused. `decode_slot`: A permutation of all slots, so each group decodes exactly 16 requests. Of one home group's requests, 0, 1 or 2 are decoded on any one group, and 2 on some group. `decode_table`: the 16 rows of one group hold each of its 128 pool pages exactly once.
All inputs are finite; a program needn't handle non-finite values.
Results may differ from the reference program's by a relative error of at most 0.012.
Values may be sent and summed in bfloat16 or wider, within the bound.
No kernel may reach another device: no remote copies, remote signals or barrier semaphores. Data moves between devices by JAX's collectives and lax.ppermute only.
A program may use at most 128 MiB of HBM per device.

```python
import math
import jax
import jax.numpy as jnp
from jax import lax

HEADS = 64
KVH = 8
HD = 128
PAGE = 64
STEPS = 4
MAXP = 8
REQ_G = 16
REQS = 256
CAP_R = 2
CAP_P = 14
PAGES_G = 96
POOL = 128


def one_order(order_key):
    return jax.random.permutation(order_key, REQ_G).astype(jnp.int32)


def pool_order(order_key):
    return jax.random.permutation(order_key, POOL).astype(jnp.int32)


def slot_layout(key):
    key = jax.random.fold_in(key, 13)
    group_count = REQS // REQ_G
    half_count = group_count // 2
    key_home, key_dest, key_shift, key_slots, key_order = jax.random.split(key, 5)
    home_label = jax.random.permutation(key_home, group_count).astype(jnp.int32)
    dest_label = jax.random.permutation(key_dest, group_count).astype(jnp.int32)
    offset_groups = jax.random.randint(key_shift, (), 1, half_count)
    circle = (dest_label[None, :] - home_label[:, None]) % group_count
    second = (circle - offset_groups) % group_count
    pair_counts = CAP_R // 2 * ((circle < half_count).astype(jnp.int32) + (second < half_count).astype(jnp.int32))
    running = jnp.cumsum(pair_counts, axis=1)
    item_index = jnp.arange(REQ_G, dtype=jnp.int32)
    target = jnp.sum((running[:, None, :] <= item_index[None, :, None]).astype(jnp.int32), axis=2)
    row_start = running - pair_counts
    column_start = jnp.cumsum(pair_counts, axis=0) - pair_counts
    is_target = target[:, :, None] == jnp.arange(group_count, dtype=jnp.int32)[None, None, :]
    arrival = jnp.sum(jnp.where(is_target, column_start[:, None, :] + item_index[None, :, None] - row_start[:, None, :], 0), axis=2)
    slot_orders = jax.vmap(one_order)(jax.random.split(key_slots, group_count))
    slot_here = slot_orders[target, arrival]
    global_slot = target * REQ_G + slot_here
    request_orders = jax.vmap(one_order)(jax.random.split(key_order, group_count))
    result = jnp.zeros((group_count, REQ_G), jnp.int32).at[jnp.arange(group_count, dtype=jnp.int32)[:, None], request_orders].set(global_slot)
    return result.reshape(REQS).astype(jnp.int32)


def page_layout(key):
    slots = slot_layout(key)
    key = jax.random.fold_in(key, 17)
    group_count = REQS // REQ_G
    extra_pages = MAXP - 1
    item_count = REQ_G * extra_pages
    dest_rows = (slots // REQ_G).reshape(group_count, REQ_G).astype(jnp.int32)

    def one_group(group_key, dest_row):
        key_star, key_rank, key_full, key_tail, key_pages, key_pick = jax.random.split(group_key, 6)
        group_ids = jnp.arange(group_count, dtype=jnp.int32)
        per_dest = jnp.sum((dest_row[:, None] == group_ids[None, :]).astype(jnp.int32), axis=0)
        cap_pages = jnp.where(per_dest == CAP_R, CAP_P, per_dest * MAXP)
        spare = cap_pages - per_dest
        dest_rank = jax.random.permutation(key_star, group_count).astype(jnp.int32)
        forced_dest = jnp.argmax(jnp.where(per_dest == CAP_R, dest_rank + 1, 0)).astype(jnp.int32)
        req_rank = jax.random.permutation(key_pick, REQ_G).astype(jnp.int32)
        full_request = jnp.argmax(jnp.where(dest_row == forced_dest, req_rank + 1, 0)).astype(jnp.int32)
        holder = jnp.arange(item_count, dtype=jnp.int32) // extra_pages
        item_dest = dest_row[holder]
        ranked = jax.random.permutation(key_rank, item_count).astype(jnp.int32)
        priority = jnp.where(holder == full_request, ranked - item_count, ranked)
        same = item_dest[None, :] == item_dest[:, None]
        within = jnp.sum((same & (priority[None, :] < priority[:, None])).astype(jnp.int32), axis=1)
        eligible = within < spare[item_dest]
        score = jnp.where(eligible, jnp.where(item_dest == forced_dest, ranked - 2 * item_count, ranked), ranked + 2 * item_count)
        ordering = jnp.argsort(score, stable=True)
        placed = jnp.zeros((item_count,), jnp.int32).at[ordering].set(jnp.arange(item_count, dtype=jnp.int32))
        taken_items = (placed < PAGES_G - REQ_G).astype(jnp.int32)
        owner_match = holder[None, :] == jnp.arange(REQ_G, dtype=jnp.int32)[:, None]
        page_counts = 1 + jnp.sum(jnp.where(owner_match, taken_items[None, :], 0), axis=1)
        short_tail = jax.random.randint(key_full, (REQ_G,), 1, PAGE - STEPS + 1)
        any_tail = jax.random.randint(key_tail, (REQ_G,), 1, PAGE + 1)
        tail_tokens = jnp.where(page_counts == MAXP, short_tail, any_tail)
        tail_tokens = jnp.where(jnp.arange(REQ_G) == full_request, PAGE - STEPS, tail_tokens)
        context = (page_counts - 1) * PAGE + tail_tokens
        shuffled = jax.random.permutation(key_pages, PAGES_G).astype(jnp.int32)
        offsets = jnp.cumsum(page_counts) - page_counts
        page_spots = (offsets[:, None] + jnp.arange(MAXP, dtype=jnp.int32)[None, :]) % PAGES_G
        return (context.astype(jnp.int32), shuffled[page_spots])
    context, tables = jax.vmap(one_group)(jax.random.split(key, group_count), dest_rows)
    return (context.reshape(REQS).astype(jnp.int32), tables.reshape(REQS, MAXP).astype(jnp.int32))


def token_parts(key):
    key_base = jax.random.fold_in(key, 0)
    base_values = jnp.clip(jax.random.normal(key_base, (REQS, STEPS, KVH, 2, HD)), -6.0, 6.0)
    return base_values


def draw_lengths(key, part):
    shared = page_layout(key)
    return shared[0]


def draw_owner_table(key, part):
    shared = page_layout(key)
    return shared[1]


def draw_decode_slot(key, part):
    shared = slot_layout(key)
    return shared


def draw_decode_table(key, part):
    key = jax.random.fold_in(key, 4)
    group_count = REQS // REQ_G
    orders = jax.vmap(pool_order)(jax.random.split(key, group_count))
    return orders.reshape(REQS, MAXP).astype(jnp.int32)


def draw_fresh(key, part):
    key = jax.random.fold_in(key, 5)
    key_base, key_scale = jax.random.split(key)
    page_total = REQS // REQ_G * PAGES_G
    shape_split = (page_total, KVH, PAGE, 2, HD)
    token_scale = jnp.exp(jax.random.uniform(key_scale, (page_total, KVH, PAGE, 2, 1), minval=math.log(0.3), maxval=math.log(3.0)))
    base_values = jnp.clip(jax.random.normal(key_base, shape_split), -6.0, 6.0)
    return (base_values * token_scale).reshape(page_total, KVH, PAGE, 2 * HD).astype(jnp.bfloat16)


def draw_new_kv(key, part):
    base_values = token_parts(key)
    return base_values.reshape(REQS, STEPS, KVH * 2 * HD).astype(jnp.bfloat16)


def draw_queries(key, part):
    key = jax.random.fold_in(key, 9)
    group_heads = HEADS // KVH
    values = jnp.clip(jax.random.normal(key, (REQS, STEPS, KVH, group_heads, HD)), -6.0, 6.0)
    return values.reshape(REQS, STEPS, HEADS * HD).astype(jnp.bfloat16)


def setup_inputs(seed: int = 0) -> dict:
    splits = jax.random.split(jax.random.key(seed), 8)
    fresh = draw_fresh(jax.random.fold_in(splits[7], 71), 0)
    lengths = draw_lengths(jax.random.fold_in(splits[7], 71), 0)
    owner_table = draw_owner_table(jax.random.fold_in(splits[7], 71), 0)
    decode_slot = draw_decode_slot(jax.random.fold_in(splits[7], 71), 0)
    decode_table = draw_decode_table(jax.random.fold_in(splits[7], 71), 0)
    queries = draw_queries(jax.random.fold_in(splits[7], 71), 0)
    new_kv = draw_new_kv(jax.random.fold_in(splits[7], 71), 0)
    return {"fresh": fresh, "lengths": lengths, "owner_table": owner_table, "decode_slot": decode_slot, "decode_table": decode_table, "queries": queries, "new_kv": new_kv}


def token_mask(tile_set, lengths_in, page_len):
    maxpages = tile_set.shape[1]
    position = jnp.arange(maxpages)[:, None] * page_len + jnp.arange(page_len)[None, :]
    inside = position[None, :, :] < lengths_in[:, None, None]
    return jnp.where(inside[:, :, None, :, None], tile_set, jnp.zeros((), tile_set.dtype))


def page_tiles(page_store, table_rows, lengths_in, page_len):
    shaped = (table_rows.shape[0], table_rows.shape[1]) + page_store.shape[1:]
    picked = jnp.take(page_store, table_rows.reshape(-1), axis=0).reshape(shaped)
    return token_mask(picked, lengths_in, page_len)


def append_tokens(tile_set, new_rows, lengths_in, page_len):
    row_count = new_rows.shape[0]
    step_count = new_rows.shape[1]
    tokens = new_rows.reshape(row_count, step_count, tile_set.shape[2], tile_set.shape[4])
    target = lengths_in[:, None] + jnp.arange(step_count, dtype=jnp.int32)[None, :]
    row_index = jnp.arange(row_count, dtype=jnp.int32)[:, None]
    return tile_set.at[row_index, target // page_len, :, target % page_len, :].set(tokens)


def attend(query_rows, tile_set, lengths_in, group_heads):
    row_count, step_count, row_width = query_rows.shape
    maxpages, kv_heads, page_len, doubled = tile_set.shape[1:]
    head_dim = doubled // 2
    shaped = query_rows.reshape(row_count, step_count, kv_heads, group_heads, head_dim).astype(jnp.float32)
    key_part = tile_set[..., :head_dim].astype(jnp.float32)
    value_part = tile_set[..., head_dim:].astype(jnp.float32)
    scores = jnp.einsum("rskgd,rjkpd->rkgsjp", shaped, key_part)
    scores = scores * (head_dim ** -0.5)
    position = jnp.arange(maxpages)[:, None] * page_len + jnp.arange(page_len)[None, :]
    horizon = lengths_in[:, None] + jnp.arange(step_count)[None, :] + 1
    inside = position[None, None, :, :] < horizon[:, :, None, None]
    scores = jnp.where(inside[:, None, None], scores, -jnp.inf)
    highest = jnp.max(scores, axis=(4, 5), keepdims=True)
    weights = jnp.exp(scores - highest)
    totals = jnp.sum(weights, axis=(4, 5), keepdims=True)
    soft_weights = (weights / totals).astype(jnp.bfloat16)
    mixture = jnp.einsum("rkgsjp,rjkpd->rskgd", soft_weights.astype(jnp.float32), value_part)
    return mixture.astype(jnp.bfloat16).reshape(row_count, step_count, row_width)


def reference(fresh, lengths, owner_table, decode_slot, decode_table, queries, new_kv):
    slot_count = lengths.shape[0]
    group_count = slot_count // REQ_G
    request = jnp.zeros((slot_count,), jnp.int32).at[decode_slot].set(jnp.arange(slot_count, dtype=jnp.int32))
    page_rows = owner_table[request] + ((request // REQ_G) * PAGES_G)[:, None]
    slot_len = lengths[request]

    def one_group(group_id):
        first_row = (group_id * REQ_G).astype(jnp.int32)
        rows_here = lax.dynamic_slice_in_dim(page_rows, first_row, REQ_G, 0)
        len_here = lax.dynamic_slice_in_dim(slot_len, first_row, REQ_G, 0)
        table_here = lax.dynamic_slice_in_dim(decode_table, first_row, REQ_G, 0)
        ask_here = lax.dynamic_slice_in_dim(queries, first_row, REQ_G, 0)
        new_here = lax.dynamic_slice_in_dim(new_kv, first_row, REQ_G, 0)
        tile_set = page_tiles(fresh, rows_here, len_here, PAGE)
        tile_set = append_tokens(tile_set, new_here, len_here, PAGE)
        flat_shape = (REQ_G * MAXP,) + tile_set.shape[2:]
        pool_here = jnp.zeros(flat_shape, tile_set.dtype).at[table_here.reshape(-1)].set(tile_set.reshape(flat_shape))
        return pool_here, attend(ask_here, tile_set, len_here, HEADS // KVH)

    pool_blocks, outputs = lax.map(one_group, jnp.arange(group_count, dtype=jnp.int32))
    page_pool = pool_blocks.reshape((group_count * REQ_G * MAXP,) + pool_blocks.shape[2:])
    return page_pool, outputs.reshape(slot_count, STEPS, HEADS * HD)
```

```python
import functools

import jax
import jax.numpy as jnp
from jax import lax
from jax.experimental import pallas as pl
from jax.experimental.pallas import tpu as pltpu
from jax.sharding import PartitionSpec as P

HEADS = 64
KVH = 8
HD = 128
PAGE = 64
STEPS = 4
MAXP = 8
REQ_G = 16
GROUPS = 16
TP = 8
PAGES_D = 12
ROWS = 8
ROW_TILES = PAGE // ROWS
TILES = PAGES_D + 1
ENTRIES = REQ_G * MAXP
GH = HEADS // KVH


def cut_kernel(fresh_ref, meta_ref, out_ref):
    for half in range(2):
        for head in range(KVH):
            row = half * KVH + head
            for page in range(PAGES_D):
                out_ref[row, page] = fresh_ref[page, head, 0, :, half * HD:(half + 1) * HD]
            out_ref[row, PAGES_D] = meta_ref[...]


def cut(fresh, meta):
    return pl.pallas_call(
        cut_kernel,
        grid=(ROW_TILES,),
        in_specs=[
            pl.BlockSpec((PAGES_D, KVH, 1, ROWS, 2 * HD), lambda i: (0, 0, i, 0, 0)),
            pl.BlockSpec((ROWS, HD), lambda i: (0, 0)),
        ],
        out_specs=pl.BlockSpec((2 * KVH, TILES, ROWS, HD), lambda i: (i, 0, 0, 0)),
        out_shape=jax.ShapeDtypeStruct((GROUPS * TP, TILES, ROWS, HD), jnp.bfloat16),
        name="cut",
    )(fresh, meta)


def pick_kernel(got_ref, out_ref, len_ref, ints, table, sem):
    for home in range(GROUPS):
        tile = got_ref[home * TP * TILES + PAGES_D]
        ints[pl.ds(home * ROWS, ROWS), :] = tile.astype(jnp.float32).astype(jnp.int32)
    copy = pltpu.make_async_copy(ints, table, sem)
    copy.start()
    copy.wait()

    def one_home(home, carry):
        row = home * ROWS
        base = home * (TP * TILES)
        for item in range(REQ_G):
            slot = table[row + 2, REQ_G + item] * REQ_G + table[row + 3, REQ_G + item]
            len_ref[slot] = table[row + 1, REQ_G + item] * PAGE + table[row, REQ_G + item]
            for j in range(MAXP):
                out_ref[slot * MAXP + j] = got_ref[base + table[row + j, item]]
        return carry

    lax.fori_loop(0, GROUPS, one_home, 0)


def pick(got):
    return pl.pallas_call(
        pick_kernel,
        in_specs=[pl.BlockSpec(memory_space=pltpu.VMEM)],
        out_specs=[
            pl.BlockSpec(memory_space=pltpu.VMEM),
            pl.BlockSpec(memory_space=pltpu.SMEM),
        ],
        out_shape=[
            jax.ShapeDtypeStruct((GROUPS * ENTRIES, ROWS, HD), jnp.bfloat16),
            jax.ShapeDtypeStruct((GROUPS * REQ_G,), jnp.int32),
        ],
        scratch_shapes=[
            pltpu.VMEM((GROUPS * ROWS, HD), jnp.int32),
            pltpu.SMEM((GROUPS * ROWS, HD), jnp.int32),
            pltpu.SemaphoreType.DMA,
        ],
        compiler_params=pltpu.CompilerParams(vmem_limit_bytes=40 * 1024 * 1024),
        name="pick",
    )(got)


def serve_kernel(len_ref, table_ref, arrived_ref, query_ref, new_ref, pool_ref, out_ref, tiles, sems):
    slot = pl.program_id(0)
    buf = lax.rem(slot, 2)
    length = len_ref[slot]

    def page_copy(which, j):
        at = lax.rem(which, 2)
        return pltpu.make_async_copy(
            tiles.at[at, j], pool_ref.at[table_ref[which * MAXP + j]], sems.at[at, j]
        )

    @pl.when(slot >= 2)
    def _():
        for j in range(MAXP):
            page_copy(slot - 2, j).wait()

    row = lax.broadcasted_iota(jnp.int32, (ROWS, HD), 0)
    fresh_rows = new_ref[0].astype(jnp.float32)
    for j in range(MAXP):
        for rt in range(ROW_TILES):
            at = row + (j * PAGE + rt * ROWS) - length
            for half in range(2):
                lanes = slice(half * HD, (half + 1) * HD)
                x = arrived_ref[2 * rt + half, 0, j].astype(jnp.float32)
                x = jnp.where(at < 0, x, 0.0)
                for u in range(STEPS):
                    x = jnp.where(at == u, fresh_rows[u:u + 1, lanes], x)
                tiles[buf, j, rt, :, lanes] = x.astype(jnp.bfloat16)
    for j in range(MAXP):
        page_copy(slot, j).start()

    span = MAXP * PAGE
    key = tiles[buf, :, :, :, :HD].reshape(span, HD)
    value = tiles[buf, :, :, :, HD:].reshape(span, HD)
    query = query_ref[0]
    scores = lax.dot_general(
        query, key, (((1,), (1,)), ((), ())), preferred_element_type=jnp.float32
    ) * (HD ** -0.5)
    step = lax.rem(lax.broadcasted_iota(jnp.int32, (GH * STEPS, span), 0), STEPS)
    where = lax.broadcasted_iota(jnp.int32, (GH * STEPS, span), 1)
    scores = jnp.where(where < length + step + 1, scores, -jnp.inf)
    highest = jnp.max(scores, axis=1, keepdims=True)
    weights = jnp.exp(scores - highest)
    totals = jnp.sum(weights, axis=1, keepdims=True)
    probs = (weights / totals).astype(jnp.bfloat16)
    mixed = jnp.dot(probs, value, preferred_element_type=jnp.float32).astype(jnp.bfloat16)
    for g in range(GH):
        out_ref[0, :, g * HD:(g + 1) * HD] = mixed[g * STEPS:(g + 1) * STEPS]

    @pl.when(slot == REQ_G - 1)
    def _():
        for which in (REQ_G - 2, REQ_G - 1):
            for j in range(MAXP):
                page_copy(jnp.int32(which), j).wait()


def serve(slot_len, table, arrived, queries, new_kv):
    return pl.pallas_call(
        serve_kernel,
        grid_spec=pltpu.PrefetchScalarGridSpec(
            num_scalar_prefetch=2,
            grid=(REQ_G,),
            in_specs=[
                pl.BlockSpec((GROUPS, 1, MAXP, ROWS, HD), lambda i, *_: (0, i, 0, 0, 0)),
                pl.BlockSpec((1, GH * STEPS, HD), lambda i, *_: (i, 0, 0)),
                pl.BlockSpec((1, STEPS, 2 * HD), lambda i, *_: (i, 0, 0)),
            ],
            out_specs=[
                pl.BlockSpec(memory_space=pl.ANY),
                pl.BlockSpec((1, STEPS, GH * HD), lambda i, *_: (i, 0, 0)),
            ],
            scratch_shapes=[
                pltpu.VMEM((2, MAXP, ROW_TILES, ROWS, 2 * HD), jnp.bfloat16),
                pltpu.SemaphoreType.DMA((2, MAXP)),
            ],
        ),
        out_shape=[
            jax.ShapeDtypeStruct((ENTRIES, ROW_TILES, ROWS, 2 * HD), jnp.bfloat16),
            jax.ShapeDtypeStruct((REQ_G, STEPS, GH * HD), jnp.bfloat16),
        ],
        compiler_params=pltpu.CompilerParams(vmem_limit_bytes=40 * 1024 * 1024),
        name="serve",
    )(slot_len, table, arrived, queries, new_kv)


def table_tile(lengths, owner_table, decode_slot):
    place = (owner_table // PAGES_D) * TILES + owner_table % PAGES_D
    facts = jnp.stack(
        [lengths % PAGE, lengths // PAGE, decode_slot // REQ_G, decode_slot % REQ_G], axis=0
    )
    facts = jnp.pad(facts, ((0, ROWS - 4), (0, HD - 2 * REQ_G)))
    return jnp.concatenate([place.T, facts], axis=1).astype(jnp.bfloat16)


def shards(fresh, lengths, owner_table, decode_slot, decode_table, queries, new_kv):
    meta = table_tile(lengths, owner_table, decode_slot)
    sent = cut(fresh.reshape(PAGES_D, KVH, ROW_TILES, ROWS, 2 * HD), meta)
    got = lax.all_to_all(sent, ("group", "tp"), split_axis=0, concat_axis=0, tiled=True)
    packed, all_len = pick(got.reshape(GROUPS * TP * TILES, ROWS, HD))
    arrived = lax.all_to_all(
        packed.reshape(GROUPS, ENTRIES, ROWS, HD), "group", split_axis=0, concat_axis=0, tiled=True
    )
    slot_len = lax.dynamic_slice_in_dim(all_len, lax.axis_index("group") * REQ_G, REQ_G, 0)
    by_head = queries.reshape(REQ_G, STEPS, GH, HD).transpose(0, 2, 1, 3)
    pool, attended = serve(
        slot_len,
        decode_table.reshape(-1),
        arrived.reshape(GROUPS, REQ_G, MAXP, ROWS, HD),
        by_head.reshape(REQ_G, GH * STEPS, HD),
        new_kv,
    )
    return pool.reshape(ENTRIES, 1, PAGE, 2 * HD), attended


def solution(mesh):
    return jax.shard_map(
        shards,
        mesh=mesh,
        in_specs=(
            P(("group", "tp"), None, None, None),
            P("group"),
            P("group", None),
            P("group"),
            P("group", None),
            P("group", None, "tp"),
            P("group", None, "tp"),
        ),
        out_specs=(P("group", "tp", None, None), P("group", None, "tp")),
        check_vma=False,
    )
```

```python
import jax
import jax.numpy as jnp
from jax import lax
from jax.experimental import pallas as pl
from jax.experimental.pallas import tpu as pltpu
from jax.sharding import PartitionSpec as P

HEADS = 64
KVH = 8
HD = 128
PAGE = 64
STEPS = 4
MAXP = 8
REQ_G = 16
GROUPS = 16
TP = 8
PAGES_D = 12
ROWS = 8
ROW_TILES = PAGE // ROWS
TILES = PAGES_D + 1
ENTRIES = REQ_G * MAXP
GH = HEADS // KVH
SPAN = MAXP * PAGE
UNROLL = 8

VMEM = pl.BlockSpec(memory_space=pltpu.VMEM)
SMEM = pl.BlockSpec(memory_space=pltpu.SMEM)
HBM = pl.BlockSpec(memory_space=pltpu.HBM)
ANY = pl.BlockSpec(memory_space=pl.ANY)
LIMIT = 40 * 1024 * 1024


def cut_kernel(fresh_ref, owner_ref, length_ref, slot_ref, out_ref, pages, owners, facts, ints, sems, table_sem):
    copies = []
    for page in range(PAGES_D):
        copy = pltpu.make_async_copy(fresh_ref.at[page], pages.at[page], sems.at[page])
        copy.start()
        copies.append(copy)
    tables = [
        pltpu.make_async_copy(owner_ref, owners, table_sem.at[0]),
        pltpu.make_async_copy(length_ref, facts.at[0], table_sem.at[1]),
        pltpu.make_async_copy(slot_ref, facts.at[1], table_sem.at[2]),
    ]
    for copy in tables:
        copy.start()

    for page in range(PAGES_D):
        copies[page].wait()
        for rt in range(ROW_TILES):
            for half in range(2):
                for head in range(KVH):
                    row = (rt * 2 + half) * KVH + head
                    out_ref[row, page] = pages[page, head, rt, :, half * HD:(half + 1) * HD]

    for copy in tables:
        copy.wait()
    owner = owners[...]
    device = (owner * 43) >> 9
    place = device * TILES + (owner - device * PAGES_D)
    length = facts[0]
    ints[...] = jnp.zeros_like(ints)
    for j in range(MAXP):
        ints[0:1, j * REQ_G:(j + 1) * REQ_G] = place[j:j + 1, :]
    ints[1:2, :REQ_G] = length & (PAGE - 1)
    ints[2:3, :REQ_G] = length >> 6
    ints[3:4, :REQ_G] = facts[1]
    tile = ints[...].astype(jnp.float32).astype(jnp.bfloat16)
    for row in range(GROUPS * TP):
        out_ref[row, PAGES_D] = tile


def cut(fresh, owner_table, lengths, decode_slot):
    return pl.pallas_call(
        cut_kernel,
        in_specs=[HBM, HBM, HBM, HBM],
        out_specs=VMEM,
        out_shape=jax.ShapeDtypeStruct((GROUPS * TP, TILES, ROWS, HD), jnp.bfloat16),
        scratch_shapes=[
            pltpu.VMEM((PAGES_D, KVH, ROW_TILES, ROWS, 2 * HD), jnp.bfloat16),
            pltpu.VMEM((MAXP, REQ_G), jnp.int32),
            pltpu.VMEM((2, 1, REQ_G), jnp.int32),
            pltpu.VMEM((ROWS, HD), jnp.int32),
            pltpu.SemaphoreType.DMA((PAGES_D,)),
            pltpu.SemaphoreType.DMA((3,)),
        ],
        compiler_params=pltpu.CompilerParams(vmem_limit_bytes=LIMIT),
        name="cut",
    )(
        fresh.reshape(PAGES_D, KVH, ROW_TILES, ROWS, 2 * HD),
        owner_table.T,
        lengths.reshape(1, REQ_G),
        decode_slot.reshape(1, REQ_G),
    )


def pick_kernel(got_ref, out_ref, len_ref, ints, table, sem):
    for home in range(GROUPS):
        tile = got_ref[home * TP * TILES + PAGES_D].astype(jnp.float32).astype(jnp.int32)
        ints[home:home + 1, :] = tile[0:1] + home * TP * TILES
        ints[GROUPS + home:GROUPS + home + 1, :] = tile[1:2] + tile[2:3] * PAGE
        ints[2 * GROUPS + home:2 * GROUPS + home + 1, :] = tile[3:4]
    copy = pltpu.make_async_copy(ints, table, sem)
    copy.start()
    copy.wait()

    def one_home(home, carry):
        for item in range(REQ_G):
            slot = table[home + 2 * GROUPS, item]
            len_ref[slot] = table[home + GROUPS, item]
            for j in range(MAXP):
                out_ref[slot * MAXP + j] = got_ref[table[home, j * REQ_G + item]]
        return carry

    lax.fori_loop(0, GROUPS, one_home, 0)


def pick(got):
    return pl.pallas_call(
        pick_kernel,
        in_specs=[VMEM],
        out_specs=[VMEM, SMEM],
        out_shape=[
            jax.ShapeDtypeStruct((GROUPS * ENTRIES, ROWS, HD), jnp.bfloat16),
            jax.ShapeDtypeStruct((GROUPS * REQ_G,), jnp.int32),
        ],
        scratch_shapes=[
            pltpu.VMEM((3 * GROUPS, HD), jnp.int32),
            pltpu.SMEM((3 * GROUPS, HD), jnp.int32),
            pltpu.SemaphoreType.DMA,
        ],
        compiler_params=pltpu.CompilerParams(vmem_limit_bytes=LIMIT),
        name="pick",
    )(got)


def serve_kernel(len_ref, table_ref, arrived_ref, query_ref, new_ref, pool_ref, out_ref, tiles, sems):
    mine = lax.axis_index("group") * REQ_G

    def page_copy(slot, j):
        return pltpu.make_async_copy(
            tiles.at[slot, j], pool_ref.at[table_ref[j, slot]], sems.at[slot, j]
        )

    row = lax.broadcasted_iota(jnp.int32, (ROWS, HD), 0)
    wide = lax.broadcasted_iota(jnp.int32, (ROWS, 2 * HD), 0)

    def fill(slot, carry):
        length = len_ref[mine + slot]
        for j in range(MAXP):
            for rt in range(ROW_TILES):
                old = row < length - (j * PAGE + rt * ROWS)
                for half in range(2):
                    x = arrived_ref[2 * rt + half, slot, j].astype(jnp.float32)
                    x = jnp.where(old, x, 0.0).astype(jnp.bfloat16)
                    tiles[slot, j, rt, :, half * HD:(half + 1) * HD] = x
        late = new_ref[slot].astype(jnp.float32)
        for position in (length, length + STEPS - 1):
            j, rt = position // PAGE, position % PAGE // ROWS
            at = wide + (position // ROWS * ROWS - length)
            x = tiles[slot, j, rt].astype(jnp.float32)
            for u in range(STEPS):
                x = jnp.where(at == u, late[u:u + 1], x)
            tiles[slot, j, rt] = x.astype(jnp.bfloat16)
        for j in range(MAXP):
            page_copy(slot, j).start()
        return carry

    lax.fori_loop(0, REQ_G, fill, 0)

    shape = (GH * STEPS, SPAN)
    step = lax.rem(lax.broadcasted_iota(jnp.int32, shape, 0), STEPS)
    ahead = lax.broadcasted_iota(jnp.int32, shape, 1) - step - 1

    def attend(first, carry):
        slots = [first * UNROLL + k for k in range(UNROLL)]
        scores = []
        for slot in slots:
            key = tiles[slot, :, :, :, :HD].reshape(SPAN, HD)
            products = lax.dot_general(
                query_ref[slot], key, (((1,), (1,)), ((), ())), preferred_element_type=jnp.float32
            )
            scores.append(jnp.where(ahead < len_ref[mine + slot], products * (HD ** -0.5), -jnp.inf))
        highest = [jnp.max(x, axis=1, keepdims=True) for x in scores]
        weights = [jnp.exp(x - y) for x, y in zip(scores, highest)]
        totals = [jnp.sum(x, axis=1, keepdims=True) for x in weights]
        probs = [(x / y).astype(jnp.bfloat16) for x, y in zip(weights, totals)]
        for slot, prob in zip(slots, probs):
            value = tiles[slot, :, :, :, HD:].reshape(SPAN, HD)
            mixed = jnp.dot(prob, value, preferred_element_type=jnp.float32).astype(jnp.bfloat16)
            for g in range(GH):
                out_ref[slot, :, g * HD:(g + 1) * HD] = mixed[g * STEPS:(g + 1) * STEPS]
        return carry

    lax.fori_loop(0, REQ_G // UNROLL, attend, 0)

    def finish(slot, carry):
        for j in range(MAXP):
            page_copy(slot, j).wait()
        return carry

    lax.fori_loop(0, REQ_G, finish, 0)


def serve(lengths, table, arrived, queries, new_kv):
    return pl.pallas_call(
        serve_kernel,
        in_specs=[SMEM, SMEM, VMEM, VMEM, VMEM],
        out_specs=[ANY, VMEM],
        out_shape=[
            jax.ShapeDtypeStruct((ENTRIES, ROW_TILES, ROWS, 2 * HD), jnp.bfloat16),
            jax.ShapeDtypeStruct((REQ_G, STEPS, GH * HD), jnp.bfloat16),
        ],
        scratch_shapes=[
            pltpu.VMEM((REQ_G, MAXP, ROW_TILES, ROWS, 2 * HD), jnp.bfloat16),
            pltpu.SemaphoreType.DMA((REQ_G, MAXP)),
        ],
        compiler_params=pltpu.CompilerParams(vmem_limit_bytes=LIMIT),
        name="serve",
    )(lengths, table, arrived, queries, new_kv)


def shards(fresh, lengths, owner_table, decode_slot, decode_table, queries, new_kv):
    sent = cut(fresh, owner_table, lengths, decode_slot)
    got = lax.all_to_all(sent, ("group", "tp"), split_axis=0, concat_axis=0, tiled=True)
    packed, all_len = pick(got.reshape(GROUPS * TP * TILES, ROWS, HD))
    by_head = queries.reshape(REQ_G, STEPS, GH, HD).transpose(0, 2, 1, 3)
    arrived = lax.all_to_all(
        packed.reshape(GROUPS, ENTRIES, ROWS, HD), "group", split_axis=0, concat_axis=0, tiled=True
    )
    pool, attended = serve(
        all_len,
        decode_table.T,
        arrived.reshape(GROUPS, REQ_G, MAXP, ROWS, HD),
        by_head.reshape(REQ_G, GH * STEPS, HD),
        new_kv,
    )
    return pool.reshape(ENTRIES, 1, PAGE, 2 * HD), attended


def solution(mesh):
    return jax.shard_map(
        shards,
        mesh=mesh,
        in_specs=(
            P(("group", "tp"), None, None, None),
            P("group"),
            P("group", None),
            P("group"),
            P("group", None),
            P("group", None, "tp"),
            P("group", None, "tp"),
        ),
        out_specs=(P("group", "tp", None, None), P("group", None, "tp")),
        check_vma=False,
    )
```

```python
import functools

import jax
import jax.numpy as jnp
from jax import lax
from jax.experimental import pallas as pl
from jax.experimental.pallas import tpu as pltpu
from jax.sharding import PartitionSpec as P

HEADS = 64
KVH = 8
HD = 128
PAGE = 64
STEPS = 4
MAXP = 8
REQ_G = 16
GROUPS = 16
TP = 8
PAGES_D = 12
ROWS = 8
ROW_TILES = PAGE // ROWS
TILES = PAGES_D + 1
ENTRIES = REQ_G * MAXP
GH = HEADS // KVH
BLOCKS = HD // REQ_G
SLOTS = GROUPS * REQ_G
SPAN = MAXP * PAGE
USUAL = 108
UNROLL = 8

VMEM = pl.BlockSpec(memory_space=pltpu.VMEM)
SMEM = pl.BlockSpec(memory_space=pltpu.SMEM)
HBM = pl.BlockSpec(memory_space=pltpu.HBM)
ANY = pl.BlockSpec(memory_space=pl.ANY)
LIMIT = 40 * 1024 * 1024


def cut_kernel(fresh_ref, owner_ref, length_ref, slot_ref, out_ref, pages, owners, facts, ints, sems, table_sem):
    copies = []
    for page in range(PAGES_D):
        copy = pltpu.make_async_copy(fresh_ref.at[page], pages.at[page], sems.at[page])
        copy.start()
        copies.append(copy)
    tables = [
        pltpu.make_async_copy(owner_ref, owners, table_sem.at[0]),
        pltpu.make_async_copy(length_ref, facts.at[0], table_sem.at[1]),
        pltpu.make_async_copy(slot_ref, facts.at[1], table_sem.at[2]),
    ]
    for copy in tables:
        copy.start()

    for page in range(PAGES_D):
        copies[page].wait()
        for rt in range(ROW_TILES):
            for half in range(2):
                for head in range(KVH):
                    row = (rt * 2 + half) * KVH + head
                    out_ref[row, page] = pages[page, head, rt, :, half * HD:(half + 1) * HD]

    for copy in tables:
        copy.wait()
    owner = owners[...]
    device = (owner * 43) >> 9
    place = device * TILES + (owner - device * PAGES_D)
    length = facts[0]
    ints[...] = jnp.zeros_like(ints)
    for block in range(BLOCKS):
        lanes = slice(block * REQ_G, (block + 1) * REQ_G)
        ints[:ROWS, lanes] = place
        ints[ROWS:ROWS + 1, lanes] = length & (PAGE - 1)
        ints[ROWS + 1:ROWS + 2, lanes] = length >> 6
        ints[ROWS + 2:ROWS + 3, lanes] = facts[1]
    block = lax.broadcasted_iota(jnp.int32, (ROWS, HD), 1) // REQ_G
    mine = lax.rem(lax.axis_index("group"), BLOCKS)
    tile = jnp.where(block == mine, ints[:ROWS], 0)
    tile = jnp.where(block == lax.rem(mine + 1, BLOCKS), ints[ROWS:], tile)
    tile = tile.astype(jnp.float32).astype(jnp.bfloat16)
    for row in range(GROUPS * TP):
        out_ref[row, PAGES_D] = tile


def cut(fresh, owner_table, lengths, decode_slot):
    return pl.pallas_call(
        cut_kernel,
        in_specs=[HBM, HBM, HBM, HBM],
        out_specs=VMEM,
        out_shape=jax.ShapeDtypeStruct((GROUPS * TP, TILES, ROWS, HD), jnp.bfloat16),
        scratch_shapes=[
            pltpu.VMEM((PAGES_D, KVH, ROW_TILES, ROWS, 2 * HD), jnp.bfloat16),
            pltpu.VMEM((MAXP, REQ_G), jnp.int32),
            pltpu.VMEM((2, 1, REQ_G), jnp.int32),
            pltpu.VMEM((2 * ROWS, HD), jnp.int32),
            pltpu.SemaphoreType.DMA((PAGES_D,)),
            pltpu.SemaphoreType.DMA((3,)),
        ],
        compiler_params=pltpu.CompilerParams(vmem_limit_bytes=60078000),
        name="cut",
    )(
        fresh.reshape(PAGES_D, KVH, ROW_TILES, ROWS, 2 * HD),
        owner_table.T,
        lengths.reshape(1, REQ_G),
        decode_slot.reshape(1, REQ_G),
    )


def pick_kernel(cap, got_ref, out_ref, len_ref, over_ref, ints, table, sem):
    block = lax.broadcasted_iota(jnp.int32, (ROWS, HD), 1) // REQ_G
    which = lax.broadcasted_iota(jnp.int32, (SLOTS, HD), 0).astype(jnp.float32)
    sorted_rows = jnp.zeros((2 * ROWS, SLOTS), jnp.float32)
    for half in range(GROUPS // BLOCKS):
        place = jnp.zeros((ROWS, HD), jnp.float32)
        facts = jnp.zeros((ROWS, HD), jnp.float32)
        for k in range(BLOCKS):
            tile = got_ref[(half * BLOCKS + k) * TP * TILES + PAGES_D].astype(jnp.float32)
            place = jnp.where(block == k, tile, place)
            facts = jnp.where(block == (k + 1) % BLOCKS, tile, facts)
        facts = pltpu.roll(facts, HD - REQ_G, 1)
        home = (block + half * BLOCKS).astype(jnp.float32)
        rows = jnp.concatenate([place, facts[0:2], home[0:6]], axis=0).astype(jnp.bfloat16)
        here = jnp.where(facts[2:3] == which, 1.0, 0.0).astype(jnp.bfloat16)
        sorted_rows += lax.dot_general(
            rows, here, (((1,), (1,)), ((), ())), preferred_element_type=jnp.float32
        )
    sorted_rows = sorted_rows.astype(jnp.int32)
    length = sorted_rows[8:9] + sorted_rows[9:10] * PAGE
    count = (length + PAGE - 1) >> 6
    slot = lax.broadcasted_iota(jnp.int32, (ROWS, SLOTS), 1)
    first = jnp.broadcast_to(count, (ROWS, SLOTS))
    for step in (1, 2, 4, 8):
        first += jnp.where(slot % REQ_G >= step, pltpu.roll(first, step, 1), 0)
    over = jnp.where(first > cap, 1.0, 0.0)
    ints[:ROWS] = sorted_rows[:ROWS] + sorted_rows[10:11] * (TP * TILES)
    ints[ROWS:] = first - count + slot // REQ_G * cap
    copy = pltpu.make_async_copy(ints, table, sem)
    copy.start()
    len_ref[...] = length
    over_ref[0] = jnp.max(over).astype(jnp.int32)
    copy.wait()

    def fill(group, clamp):
        for item in range(REQ_G):
            at = table[ROWS, group * REQ_G + item]
            for j in reversed(range(MAXP)):
                place = at + j
                if clamp:
                    place = jnp.minimum(place, GROUPS * cap - 1)
                out_ref[place] = got_ref[table[j, group * REQ_G + item]]

    def one_group(group, carry):
        fill(group, False)
        return carry

    lax.fori_loop(0, GROUPS - 1, one_group, 0)
    fill(GROUPS - 1, True)


def pick(got, cap):
    return pl.pallas_call(
        functools.partial(pick_kernel, cap),
        in_specs=[VMEM],
        out_specs=[VMEM, VMEM, SMEM],
        out_shape=[
            jax.ShapeDtypeStruct((GROUPS * cap, ROWS, HD), jnp.bfloat16),
            jax.ShapeDtypeStruct((1, SLOTS), jnp.int32),
            jax.ShapeDtypeStruct((1,), jnp.int32),
        ],
        scratch_shapes=[
            pltpu.VMEM((2 * ROWS, SLOTS), jnp.int32),
            pltpu.SMEM((2 * ROWS, SLOTS), jnp.int32),
            pltpu.SemaphoreType.DMA,
        ],
        compiler_params=pltpu.CompilerParams(vmem_limit_bytes=LIMIT),
        name="pick",
    )(got)


def serve_kernel(cap, len_ref, table_ref, arrived_ref, query_ref, new_ref, pool_ref, out_ref, tiles, sem):
    mine = lax.axis_index("group") * REQ_G

    def page_copy(slot, j):
        return pltpu.make_async_copy(
            tiles.at[slot * MAXP + j], pool_ref.at[table_ref[j, slot]], sem
        )

    row = lax.broadcasted_iota(jnp.int32, (ROWS, HD), 0)
    wide = lax.broadcasted_iota(jnp.int32, (ROWS, 2 * HD), 0)

    def fill(slot, first):
        length = len_ref[0, mine + slot]
        for j in range(MAXP):
            entry = jnp.minimum(first + j, cap - 1)
            for rt in range(ROW_TILES):
                old = row < length - (j * PAGE + rt * ROWS)
                for half in range(2):
                    x = arrived_ref[2 * rt + half, entry].astype(jnp.float32)
                    x = jnp.where(old, x, 0.0).astype(jnp.bfloat16)
                    tiles[slot * MAXP + j, rt, :, half * HD:(half + 1) * HD] = x
        late = new_ref[slot].astype(jnp.float32)
        for position in (length, length + STEPS - 1):
            j, rt = position // PAGE, position % PAGE // ROWS
            at = wide + (position // ROWS * ROWS - length)
            x = tiles[slot * MAXP + j, rt].astype(jnp.float32)
            for u in range(STEPS):
                x = jnp.where(at == u, late[u:u + 1], x)
            tiles[slot * MAXP + j, rt] = x.astype(jnp.bfloat16)
        for j in range(MAXP):
            page_copy(slot, j).start()
        return first + ((length + PAGE - 1) >> 6)

    lax.fori_loop(0, REQ_G, fill, jnp.int32(0))

    shape = (GH * STEPS, SPAN)
    step = lax.rem(lax.broadcasted_iota(jnp.int32, shape, 0), STEPS)
    ahead = lax.broadcasted_iota(jnp.int32, shape, 1) - step - 1

    def attend(first, carry):
        slots = [first * UNROLL + k for k in range(UNROLL)]
        scores = []
        for slot in slots:
            key = tiles[pl.ds(slot * MAXP, MAXP), :, :, :HD].reshape(SPAN, HD)
            products = lax.dot_general(
                query_ref[slot], key, (((1,), (1,)), ((), ())), preferred_element_type=jnp.float32
            )
            scores.append(jnp.where(ahead < len_ref[0, mine + slot], products * (HD ** -0.5), -jnp.inf))
        highest = [jnp.max(x, axis=1, keepdims=True) for x in scores]
        weights = [jnp.exp(x - y) for x, y in zip(scores, highest)]
        totals = [jnp.sum(x, axis=1, keepdims=True) for x in weights]
        probs = [(x / y).astype(jnp.bfloat16) for x, y in zip(weights, totals)]
        for slot, prob in zip(slots, probs):
            value = tiles[pl.ds(slot * MAXP, MAXP), :, :, HD:].reshape(SPAN, HD)
            mixed = jnp.dot(prob, value, preferred_element_type=jnp.float32).astype(jnp.bfloat16)
            for g in range(GH):
                out_ref[slot, :, g * HD:(g + 1) * HD] = mixed[g * STEPS:(g + 1) * STEPS]
        return carry

    lax.fori_loop(0, REQ_G // UNROLL, attend, 0)

    pltpu.make_async_copy(tiles, pool_ref, sem).wait()


def serve(lengths, table, arrived, queries, new_kv):
    return pl.pallas_call(
        functools.partial(serve_kernel, arrived.shape[1]),
        in_specs=[SMEM, SMEM, VMEM, VMEM, VMEM],
        out_specs=[ANY, VMEM],
        out_shape=[
            jax.ShapeDtypeStruct((ENTRIES, ROW_TILES, ROWS, 2 * HD), jnp.bfloat16),
            jax.ShapeDtypeStruct((REQ_G, STEPS, GH * HD), jnp.bfloat16),
        ],
        scratch_shapes=[
            pltpu.VMEM((ENTRIES, ROW_TILES, ROWS, 2 * HD), jnp.bfloat16),
            pltpu.SemaphoreType.DMA,
        ],
        compiler_params=pltpu.CompilerParams(vmem_limit_bytes=LIMIT),
        name="serve",
    )(lengths, table, arrived, queries, new_kv)


def shards(fresh, lengths, owner_table, decode_slot, decode_table, queries, new_kv):
    sent = cut(fresh, owner_table, lengths, decode_slot)
    got = lax.all_to_all(sent, ("group", "tp"), split_axis=0, concat_axis=0, tiled=True)
    got = got.reshape(GROUPS * TP * TILES, ROWS, HD)
    table = decode_table.T
    by_head = queries.reshape(REQ_G, STEPS, GH, HD).transpose(0, 2, 1, 3)
    by_head = by_head.reshape(REQ_G, GH * STEPS, HD)

    def deliver(packed, all_len, cap):
        arrived = lax.all_to_all(
            packed.reshape(GROUPS, cap, ROWS, HD), "group", split_axis=0, concat_axis=0, tiled=True
        )
        return serve(all_len, table, arrived, by_head, new_kv)

    def whole(packed, all_len):
        packed, all_len, _ = pick(got, ENTRIES)
        return deliver(packed, all_len, ENTRIES)

    packed, all_len, over = pick(got, USUAL)
    pool, attended = lax.cond(
        over[0] > 0, whole, lambda packed, all_len: deliver(packed, all_len, USUAL), packed, all_len
    )
    return pool.reshape(ENTRIES, 1, PAGE, 2 * HD), attended


def solution(mesh):
    return jax.shard_map(
        shards,
        mesh=mesh,
        in_specs=(
            P(("group", "tp"), None, None, None),
            P("group"),
            P("group", None),
            P("group"),
            P("group", None),
            P("group", None, "tp"),
            P("group", None, "tp"),
        ),
        out_specs=(P("group", "tp", None, None), P("group", None, "tp")),
        check_vma=False,
    )
```

```python
import functools

import jax
import jax.numpy as jnp
from jax import lax
from jax.experimental import pallas as pl
from jax.experimental.pallas import tpu as pltpu
from jax.sharding import PartitionSpec as P

HEADS = 64
KVH = 8
HD = 128
PAGE = 64
STEPS = 4
MAXP = 8
REQ_G = 16
GROUPS = 16
TP = 8
PAGES_D = 12
ROWS = 8
ROW_TILES = PAGE // ROWS
TILES = PAGES_D + 1
ENTRIES = REQ_G * MAXP
GH = HEADS // KVH
BLOCKS = HD // REQ_G
SLOTS = GROUPS * REQ_G
SPAN = MAXP * PAGE
USUAL = 108
UNROLL = 16

VMEM = pl.BlockSpec(memory_space=pltpu.VMEM)
SMEM = pl.BlockSpec(memory_space=pltpu.SMEM)
HBM = pl.BlockSpec(memory_space=pltpu.HBM)
ANY = pl.BlockSpec(memory_space=pl.ANY)
LIMIT = 40 * 1024 * 1024


def cut_kernel(fresh_ref, table_ref, out_ref, ints):
    owner = table_ref[:MAXP]
    device = (owner * 43) >> 9
    place = device * TILES + (owner - device * PAGES_D)
    length = table_ref[MAXP:MAXP + 1]
    slot = table_ref[MAXP + 1:MAXP + 2]
    ints[...] = jnp.zeros_like(ints)
    for block in range(BLOCKS):
        lanes = slice(block * REQ_G, (block + 1) * REQ_G)
        ints[:ROWS, lanes] = place
        ints[ROWS:ROWS + 1, lanes] = length & (PAGE - 1)
        ints[ROWS + 1:ROWS + 2, lanes] = length >> 6
        ints[ROWS + 2:ROWS + 3, lanes] = slot
    block = lax.broadcasted_iota(jnp.int32, (ROWS, HD), 1) // REQ_G
    mine = lax.rem(lax.axis_index("group"), BLOCKS)
    tile = jnp.where(block == mine, ints[:ROWS], 0)
    tile = jnp.where(block == lax.rem(mine + 1, BLOCKS), ints[ROWS:], tile)
    tile = tile.astype(jnp.float32).astype(jnp.bfloat16)
    for rt in range(ROW_TILES):
        for half in range(2):
            for head in range(KVH):
                row = (rt * 2 + half) * KVH + head
                for page in range(PAGES_D):
                    out_ref[row, page] = fresh_ref[page, head, rt, :, half * HD:(half + 1) * HD]
                out_ref[row, PAGES_D] = tile


def cut(fresh, owner_table, lengths, decode_slot):
    return pl.pallas_call(
        cut_kernel,
        in_specs=[VMEM, VMEM],
        out_specs=VMEM,
        out_shape=jax.ShapeDtypeStruct((GROUPS * TP, TILES, ROWS, HD), jnp.bfloat16),
        scratch_shapes=[pltpu.VMEM((2 * ROWS, HD), jnp.int32)],
        compiler_params=pltpu.CompilerParams(vmem_limit_bytes=LIMIT),
        name="cut",
    )(
        fresh.reshape(PAGES_D, KVH, ROW_TILES, ROWS, 2 * HD),
        jnp.concatenate([owner_table.T, lengths[None], decode_slot[None]], axis=0),
    )


def pick_kernel(cap, got_ref, out_ref, len_ref, over_ref, ints, table, sem):
    block = lax.broadcasted_iota(jnp.int32, (ROWS, HD), 1) // REQ_G
    which = lax.broadcasted_iota(jnp.int32, (SLOTS, HD), 0).astype(jnp.float32)
    sorted_rows = jnp.zeros((2 * ROWS, SLOTS), jnp.float32)
    for half in range(GROUPS // BLOCKS):
        place = jnp.zeros((ROWS, HD), jnp.float32)
        facts = jnp.zeros((ROWS, HD), jnp.float32)
        for k in range(BLOCKS):
            tile = got_ref[(half * BLOCKS + k) * TP * TILES + PAGES_D].astype(jnp.float32)
            place = jnp.where(block == k, tile, place)
            facts = jnp.where(block == (k + 1) % BLOCKS, tile, facts)
        facts = pltpu.roll(facts, HD - REQ_G, 1)
        home = (block + half * BLOCKS).astype(jnp.float32)
        rows = jnp.concatenate([place, facts[0:2], home[0:6]], axis=0).astype(jnp.bfloat16)
        here = jnp.where(facts[2:3] == which, 1.0, 0.0).astype(jnp.bfloat16)
        sorted_rows += lax.dot_general(
            rows, here, (((1,), (1,)), ((), ())), preferred_element_type=jnp.float32
        )
    sorted_rows = sorted_rows.astype(jnp.int32)
    length = sorted_rows[8:9] + sorted_rows[9:10] * PAGE
    count = (length + PAGE - 1) >> 6
    slot = lax.broadcasted_iota(jnp.int32, (ROWS, SLOTS), 1)
    first = jnp.broadcast_to(count, (ROWS, SLOTS))
    for step in (1, 2, 4, 8):
        first += jnp.where(slot % REQ_G >= step, pltpu.roll(first, step, 1), 0)
    over = jnp.where(first > cap, 1.0, 0.0)
    ints[:ROWS] = sorted_rows[:ROWS] + sorted_rows[10:11] * (TP * TILES)
    ints[ROWS:] = first - count + slot // REQ_G * cap
    copies = [
        pltpu.make_async_copy(ints.at[j], table.at[pl.ds(j * SLOTS, SLOTS)], sem.at[j])
        for j in range(MAXP + 1)
    ]
    for copy in copies:
        copy.start()
    len_ref[...] = length
    over_ref[0] = jnp.max(over).astype(jnp.int32)
    for copy in copies:
        copy.wait()

    def fill(group, clamp):
        for item in range(REQ_G):
            at = table[group * REQ_G + (ROWS * SLOTS + item)]
            span = out_ref.at[pl.ds(at, MAXP)]
            for j in reversed(range(MAXP)):
                tile = got_ref[table[group * REQ_G + (j * SLOTS + item)]]
                if clamp:
                    out_ref[jnp.minimum(at + j, GROUPS * cap - 1)] = tile
                else:
                    span[j] = tile

    def one_group(group, carry):
        fill(group, False)
        return carry

    lax.fori_loop(0, GROUPS - 1, one_group, 0)
    fill(GROUPS - 1, True)


def pick(got, cap):
    return pl.pallas_call(
        functools.partial(pick_kernel, cap),
        in_specs=[VMEM],
        out_specs=[VMEM, VMEM, SMEM],
        out_shape=[
            jax.ShapeDtypeStruct((GROUPS * cap, ROWS, HD), jnp.bfloat16),
            jax.ShapeDtypeStruct((1, SLOTS), jnp.int32),
            jax.ShapeDtypeStruct((1,), jnp.int32),
        ],
        scratch_shapes=[
            pltpu.VMEM((2 * ROWS, SLOTS), jnp.int32),
            pltpu.SMEM(((MAXP + 1) * SLOTS,), jnp.int32),
            pltpu.SemaphoreType.DMA((MAXP + 1,)),
        ],
        compiler_params=pltpu.CompilerParams(vmem_limit_bytes=LIMIT),
        name="pick",
    )(got)


def serve_kernel(cap, len_ref, table_ref, arrived_ref, query_ref, new_ref, pool_ref, out_ref, tiles, sem):
    mine = lax.axis_index("group") * REQ_G

    def page_copy(slot, j):
        return pltpu.make_async_copy(
            tiles.at[slot * MAXP + j], pool_ref.at[table_ref[j, slot]], sem
        )

    row = lax.broadcasted_iota(jnp.int32, (ROWS, HD), 0)
    wide = lax.broadcasted_iota(jnp.int32, (ROWS, 2 * HD), 0)

    def fill(slot, first):
        length = len_ref[0, mine + slot]
        for j in range(MAXP):
            entry = jnp.minimum(first + j, cap - 1)
            for rt in range(ROW_TILES):
                old = row < length - (j * PAGE + rt * ROWS)
                for half in range(2):
                    x = arrived_ref[2 * rt + half, entry].astype(jnp.float32)
                    x = jnp.where(old, x, 0.0).astype(jnp.bfloat16)
                    tiles[slot * MAXP + j, rt, :, half * HD:(half + 1) * HD] = x
        late = new_ref[slot].astype(jnp.float32)
        for position in (length, length + STEPS - 1):
            j, rt = position // PAGE, position % PAGE // ROWS
            at = wide + (position // ROWS * ROWS - length)
            x = tiles[slot * MAXP + j, rt].astype(jnp.float32)
            for u in range(STEPS):
                x = jnp.where(at == u, late[u:u + 1], x)
            tiles[slot * MAXP + j, rt] = x.astype(jnp.bfloat16)
        for j in range(MAXP):
            page_copy(slot, j).start()
        return first + ((length + PAGE - 1) >> 6)

    lax.fori_loop(0, REQ_G, fill, jnp.int32(0))

    shape = (GH * STEPS, SPAN)
    step = lax.rem(lax.broadcasted_iota(jnp.int32, shape, 0), STEPS)
    ahead = lax.broadcasted_iota(jnp.int32, shape, 1) - step - 1

    def attend(first, carry):
        slots = [first * UNROLL + k for k in range(UNROLL)]
        scores = []
        for slot in slots:
            key = tiles[pl.ds(slot * MAXP, MAXP), :, :, :HD].reshape(SPAN, HD)
            products = lax.dot_general(
                query_ref[slot], key, (((1,), (1,)), ((), ())), preferred_element_type=jnp.float32
            )
            scores.append(jnp.where(ahead < len_ref[0, mine + slot], products * (HD ** -0.5), -jnp.inf))
        highest = [jnp.max(x, axis=1, keepdims=True) for x in scores]
        weights = [jnp.exp(x - y) for x, y in zip(scores, highest)]
        totals = [jnp.sum(x, axis=1, keepdims=True) for x in weights]
        probs = [(x / y).astype(jnp.bfloat16) for x, y in zip(weights, totals)]
        for slot, prob in zip(slots, probs):
            value = tiles[pl.ds(slot * MAXP, MAXP), :, :, HD:].reshape(SPAN, HD)
            mixed = jnp.dot(prob, value, preferred_element_type=jnp.float32).astype(jnp.bfloat16)
            for g in range(GH):
                out_ref[slot, :, g * HD:(g + 1) * HD] = mixed[g * STEPS:(g + 1) * STEPS]
        return carry

    lax.fori_loop(0, REQ_G // UNROLL, attend, 0)

    pltpu.make_async_copy(tiles, pool_ref, sem).wait()


def serve(lengths, table, arrived, queries, new_kv):
    return pl.pallas_call(
        functools.partial(serve_kernel, arrived.shape[1]),
        in_specs=[SMEM, SMEM, VMEM, VMEM, VMEM],
        out_specs=[ANY, VMEM],
        out_shape=[
            jax.ShapeDtypeStruct((ENTRIES, ROW_TILES, ROWS, 2 * HD), jnp.bfloat16),
            jax.ShapeDtypeStruct((REQ_G, STEPS, GH * HD), jnp.bfloat16),
        ],
        scratch_shapes=[
            pltpu.VMEM((ENTRIES, ROW_TILES, ROWS, 2 * HD), jnp.bfloat16),
            pltpu.SemaphoreType.DMA,
        ],
        compiler_params=pltpu.CompilerParams(vmem_limit_bytes=LIMIT),
        name="serve",
    )(lengths, table, arrived, queries, new_kv)


def shards(fresh, lengths, owner_table, decode_slot, decode_table, queries, new_kv):
    sent = cut(fresh, owner_table, lengths, decode_slot)
    got = lax.all_to_all(sent, ("group", "tp"), split_axis=0, concat_axis=0, tiled=True)
    got = got.reshape(GROUPS * TP * TILES, ROWS, HD)
    table = decode_table.T
    by_head = queries.reshape(REQ_G, STEPS, GH, HD).transpose(0, 2, 1, 3)
    by_head = by_head.reshape(REQ_G, GH * STEPS, HD)

    def deliver(packed, all_len, cap):
        arrived = lax.all_to_all(
            packed.reshape(GROUPS, cap, ROWS, HD), "group", split_axis=0, concat_axis=0, tiled=True
        )
        return serve(all_len, table, arrived, by_head, new_kv)

    def whole(packed, all_len):
        packed, all_len, _ = pick(got, ENTRIES)
        return deliver(packed, all_len, ENTRIES)

    packed, all_len, over = pick(got, USUAL)
    pool, attended = lax.cond(
        over[0] > 0, whole, lambda packed, all_len: deliver(packed, all_len, USUAL), packed, all_len
    )
    return pool.reshape(ENTRIES, 1, PAGE, 2 * HD), attended


def solution(mesh):
    return jax.shard_map(
        shards,
        mesh=mesh,
        in_specs=(
            P(("group", "tp"), None, None, None),
            P("group"),
            P("group", None),
            P("group"),
            P("group", None),
            P("group", None, "tp"),
            P("group", None, "tp"),
        ),
        out_specs=(P("group", "tp", None, None), P("group", None, "tp")),
        check_vma=False,
    )
```

```python
import functools

import jax
import jax.numpy as jnp
from jax import lax
from jax.experimental import pallas as pl
from jax.experimental.pallas import tpu as pltpu
from jax.sharding import PartitionSpec as P

HEADS = 64
KVH = 8
HD = 128
PAGE = 64
STEPS = 4
MAXP = 8
REQ_G = 16
GROUPS = 16
TP = 8
PAGES_D = 12
ROWS = 8
ROW_TILES = PAGE // ROWS
TILES = PAGES_D + 1
ENTRIES = REQ_G * MAXP
GH = HEADS // KVH
BLOCKS = HD // REQ_G
SLOTS = GROUPS * REQ_G
SPAN = MAXP * PAGE
USUAL = 108
UNROLL = 16

VMEM = pl.BlockSpec(memory_space=pltpu.VMEM)
SMEM = pl.BlockSpec(memory_space=pltpu.SMEM)
HBM = pl.BlockSpec(memory_space=pltpu.HBM)
ANY = pl.BlockSpec(memory_space=pl.ANY)
LIMIT = 40 * 1024 * 1024


def cut_kernel(fresh_ref, owner_ref, length_ref, slot_ref, out_ref, pages, owners, facts, ints, sems, table_sem):
    copies = []
    for page in range(PAGES_D):
        copy = pltpu.make_async_copy(fresh_ref.at[page], pages.at[page], sems.at[page])
        copy.start()
        copies.append(copy)
    tables = [
        pltpu.make_async_copy(owner_ref, owners, table_sem.at[0]),
        pltpu.make_async_copy(length_ref, facts.at[0], table_sem.at[1]),
        pltpu.make_async_copy(slot_ref, facts.at[1], table_sem.at[2]),
    ]
    for copy in tables:
        copy.start()

    for page in range(PAGES_D):
        copies[page].wait()
        for rt in range(ROW_TILES):
            for half in range(2):
                for head in range(KVH):
                    row = (rt * 2 + half) * KVH + head
                    out_ref[row, page] = pages[page, head, rt, :, half * HD:(half + 1) * HD]

    for copy in tables:
        copy.wait()
    owner = owners[...]
    device = (owner * 43) >> 9
    place = device * TILES + (owner - device * PAGES_D)
    length = facts[0]
    ints[...] = jnp.zeros_like(ints)
    for block in range(BLOCKS):
        lanes = slice(block * REQ_G, (block + 1) * REQ_G)
        ints[:ROWS, lanes] = place
        ints[ROWS:ROWS + 1, lanes] = length & (PAGE - 1)
        ints[ROWS + 1:ROWS + 2, lanes] = length >> 6
        ints[ROWS + 2:ROWS + 3, lanes] = facts[1]
    block = lax.broadcasted_iota(jnp.int32, (ROWS, HD), 1) // REQ_G
    mine = lax.rem(lax.axis_index("group"), BLOCKS)
    tile = jnp.where(block == mine, ints[:ROWS], 0)
    tile = jnp.where(block == lax.rem(mine + 1, BLOCKS), ints[ROWS:], tile)
    tile = tile.astype(jnp.float32).astype(jnp.bfloat16)
    for row in range(GROUPS * TP):
        out_ref[row, PAGES_D] = tile


def cut(fresh, owner_table, lengths, decode_slot):
    return pl.pallas_call(
        cut_kernel,
        in_specs=[HBM, HBM, HBM, HBM],
        out_specs=VMEM,
        out_shape=pltpu.VMEM((GROUPS * TP, TILES, ROWS, HD), jnp.bfloat16),
        scratch_shapes=[
            pltpu.VMEM((PAGES_D, KVH, ROW_TILES, ROWS, 2 * HD), jnp.bfloat16),
            pltpu.VMEM((MAXP, REQ_G), jnp.int32),
            pltpu.VMEM((2, 1, REQ_G), jnp.int32),
            pltpu.VMEM((2 * ROWS, HD), jnp.int32),
            pltpu.SemaphoreType.DMA((PAGES_D,)),
            pltpu.SemaphoreType.DMA((3,)),
        ],
        compiler_params=pltpu.CompilerParams(vmem_limit_bytes=58000000),
        name="cut",
    )(
        fresh.reshape(PAGES_D, KVH, ROW_TILES, ROWS, 2 * HD),
        owner_table.T,
        lengths.reshape(1, REQ_G),
        decode_slot.reshape(1, REQ_G),
    )


def pick_kernel(cap, got_ref, out_ref, len_ref, over_ref, ints, table, sem):
    block = lax.broadcasted_iota(jnp.int32, (ROWS, HD), 1) // REQ_G
    which = lax.broadcasted_iota(jnp.int32, (SLOTS, HD), 0).astype(jnp.float32)
    sorted_rows = jnp.zeros((2 * ROWS, SLOTS), jnp.float32)
    for half in range(GROUPS // BLOCKS):
        place = jnp.zeros((ROWS, HD), jnp.float32)
        facts = jnp.zeros((ROWS, HD), jnp.float32)
        for k in range(BLOCKS):
            tile = got_ref[(half * BLOCKS + k) * TP * TILES + PAGES_D].astype(jnp.float32)
            place = jnp.where(block == k, tile, place)
            facts = jnp.where(block == (k + 1) % BLOCKS, tile, facts)
        facts = pltpu.roll(facts, HD - REQ_G, 1)
        home = (block + half * BLOCKS).astype(jnp.float32)
        rows = jnp.concatenate([place, facts[0:2], home[0:6]], axis=0).astype(jnp.bfloat16)
        here = jnp.where(facts[2:3] == which, 1.0, 0.0).astype(jnp.bfloat16)
        sorted_rows += lax.dot_general(
            rows, here, (((1,), (1,)), ((), ())), preferred_element_type=jnp.float32
        )
    sorted_rows = sorted_rows.astype(jnp.int32)
    length = sorted_rows[8:9] + sorted_rows[9:10] * PAGE
    count = (length + PAGE - 1) >> 6
    slot = lax.broadcasted_iota(jnp.int32, (ROWS, SLOTS), 1)
    first = jnp.broadcast_to(count, (ROWS, SLOTS))
    for step in (1, 2, 4, 8):
        first += jnp.where(slot % REQ_G >= step, pltpu.roll(first, step, 1), 0)
    over = jnp.where(first > cap, 1.0, 0.0)
    ints[:ROWS] = sorted_rows[:ROWS] + sorted_rows[10:11] * (TP * TILES)
    ints[ROWS:] = first - count + slot // REQ_G * cap
    copies = [
        pltpu.make_async_copy(ints.at[j], table.at[pl.ds(j * SLOTS, SLOTS)], sem.at[j])
        for j in range(MAXP + 1)
    ]
    for copy in copies:
        copy.start()
    len_ref[...] = length
    over_ref[0] = jnp.max(over).astype(jnp.int32)
    for copy in copies:
        copy.wait()

    def fill(group, clamp):
        for item in range(REQ_G):
            at = table[group * REQ_G + (ROWS * SLOTS + item)]
            span = out_ref.at[pl.ds(at, MAXP)]
            for j in reversed(range(MAXP)):
                tile = got_ref[table[group * REQ_G + (j * SLOTS + item)]]
                if clamp:
                    out_ref[jnp.minimum(at + j, GROUPS * cap - 1)] = tile
                else:
                    span[j] = tile

    def one_group(group, carry):
        fill(group, False)
        return carry

    lax.fori_loop(0, GROUPS - 1, one_group, 0)
    fill(GROUPS - 1, True)


def pick(got, cap):
    return pl.pallas_call(
        functools.partial(pick_kernel, cap),
        in_specs=[VMEM],
        out_specs=[VMEM, VMEM, SMEM],
        out_shape=[
            jax.ShapeDtypeStruct((GROUPS * cap, ROWS, HD), jnp.bfloat16),
            jax.ShapeDtypeStruct((1, SLOTS), jnp.int32),
            jax.ShapeDtypeStruct((1,), jnp.int32),
        ],
        scratch_shapes=[
            pltpu.VMEM((2 * ROWS, SLOTS), jnp.int32),
            pltpu.SMEM(((MAXP + 1) * SLOTS,), jnp.int32),
            pltpu.SemaphoreType.DMA((MAXP + 1,)),
        ],
        compiler_params=pltpu.CompilerParams(vmem_limit_bytes=LIMIT),
        name="pick",
    )(got)


def serve_kernel(cap, len_ref, table_ref, arrived_ref, query_ref, new_ref, pool_ref, out_ref, tiles, sem):
    mine = lax.axis_index("group") * REQ_G

    def page_copy(slot, j):
        return pltpu.make_async_copy(
            tiles.at[slot * MAXP + j], pool_ref.at[table_ref[j, slot]], sem
        )

    row = lax.broadcasted_iota(jnp.int32, (ROWS, HD), 0)
    wide = lax.broadcasted_iota(jnp.int32, (ROWS, 2 * HD), 0)

    def fill(slot, first):
        length = len_ref[0, mine + slot]
        for j in range(MAXP):
            entry = jnp.minimum(first + j, cap - 1)
            for rt in range(ROW_TILES):
                old = row < length - (j * PAGE + rt * ROWS)
                for half in range(2):
                    x = arrived_ref[2 * rt + half, entry].astype(jnp.float32)
                    x = jnp.where(old, x, 0.0).astype(jnp.bfloat16)
                    tiles[slot * MAXP + j, rt, :, half * HD:(half + 1) * HD] = x
        late = new_ref[slot].astype(jnp.float32)
        for position in (length, length + STEPS - 1):
            j, rt = position // PAGE, position % PAGE // ROWS
            at = wide + (position // ROWS * ROWS - length)
            x = tiles[slot * MAXP + j, rt].astype(jnp.float32)
            for u in range(STEPS):
                x = jnp.where(at == u, late[u:u + 1], x)
            tiles[slot * MAXP + j, rt] = x.astype(jnp.bfloat16)
        for j in range(MAXP):
            page_copy(slot, j).start()
        return first + ((length + PAGE - 1) >> 6)

    lax.fori_loop(0, REQ_G, fill, jnp.int32(0))

    shape = (GH * STEPS, SPAN)
    step = lax.rem(lax.broadcasted_iota(jnp.int32, shape, 0), STEPS)
    ahead = lax.broadcasted_iota(jnp.int32, shape, 1) - step - 1

    def attend(first, carry):
        slots = [first * UNROLL + k for k in range(UNROLL)]
        scores = []
        for slot in slots:
            key = tiles[pl.ds(slot * MAXP, MAXP), :, :, :HD].reshape(SPAN, HD)
            products = lax.dot_general(
                query_ref[slot], key, (((1,), (1,)), ((), ())), preferred_element_type=jnp.float32
            )
            scores.append(jnp.where(ahead < len_ref[0, mine + slot], products * (HD ** -0.5), -jnp.inf))
        highest = [jnp.max(x, axis=1, keepdims=True) for x in scores]
        weights = [jnp.exp(x - y) for x, y in zip(scores, highest)]
        totals = [jnp.sum(x, axis=1, keepdims=True) for x in weights]
        probs = [(x / y).astype(jnp.bfloat16) for x, y in zip(weights, totals)]
        for slot, prob in zip(slots, probs):
            value = tiles[pl.ds(slot * MAXP, MAXP), :, :, HD:].reshape(SPAN, HD)
            mixed = jnp.dot(prob, value, preferred_element_type=jnp.float32).astype(jnp.bfloat16)
            for g in range(GH):
                out_ref[slot, :, g * HD:(g + 1) * HD] = mixed[g * STEPS:(g + 1) * STEPS]
        return carry

    lax.fori_loop(0, REQ_G // UNROLL, attend, 0)

    pltpu.make_async_copy(tiles, pool_ref, sem).wait()


def serve(lengths, table, arrived, queries, new_kv):
    return pl.pallas_call(
        functools.partial(serve_kernel, arrived.shape[1]),
        in_specs=[SMEM, SMEM, VMEM, VMEM, VMEM],
        out_specs=[ANY, VMEM],
        out_shape=[
            jax.ShapeDtypeStruct((ENTRIES, ROW_TILES, ROWS, 2 * HD), jnp.bfloat16),
            jax.ShapeDtypeStruct((REQ_G, STEPS, GH * HD), jnp.bfloat16),
        ],
        scratch_shapes=[
            pltpu.VMEM((ENTRIES, ROW_TILES, ROWS, 2 * HD), jnp.bfloat16),
            pltpu.SemaphoreType.DMA,
        ],
        compiler_params=pltpu.CompilerParams(vmem_limit_bytes=LIMIT),
        name="serve",
    )(lengths, table, arrived, queries, new_kv)


def shards(fresh, lengths, owner_table, decode_slot, decode_table, queries, new_kv):
    sent = cut(fresh, owner_table, lengths, decode_slot)
    got = lax.all_to_all(sent, ("group", "tp"), split_axis=0, concat_axis=0, tiled=True)
    got = got.reshape(GROUPS * TP * TILES, ROWS, HD)
    table = decode_table.T
    by_head = queries.reshape(REQ_G, STEPS, GH, HD).transpose(0, 2, 1, 3)
    by_head = by_head.reshape(REQ_G, GH * STEPS, HD)

    def deliver(packed, all_len, cap):
        arrived = lax.all_to_all(
            packed.reshape(GROUPS, cap, ROWS, HD), "group", split_axis=0, concat_axis=0, tiled=True
        )
        return serve(all_len, table, arrived, by_head, new_kv)

    def whole(packed, all_len):
        packed, all_len, _ = pick(got, ENTRIES)
        return deliver(packed, all_len, ENTRIES)

    packed, all_len, over = pick(got, USUAL)
    pool, attended = lax.cond(
        over[0] > 0, whole, lambda packed, all_len: deliver(packed, all_len, USUAL), packed, all_len
    )
    return pool.reshape(ENTRIES, 1, PAGE, 2 * HD), attended


def solution(mesh):
    return jax.shard_map(
        shards,
        mesh=mesh,
        in_specs=(
            P(("group", "tp"), None, None, None),
            P("group"),
            P("group", None),
            P("group"),
            P("group", None),
            P("group", None, "tp"),
            P("group", None, "tp"),
        ),
        out_specs=(P("group", "tp", None, None), P("group", None, "tp")),
        check_vma=False,
    )
```

```python
import functools

import jax
import jax.numpy as jnp
from jax import lax
from jax.experimental import pallas as pl
from jax.experimental.pallas import tpu as pltpu
from jax.sharding import PartitionSpec as P

HEADS = 64
KVH = 8
HD = 128
PAGE = 64
STEPS = 4
MAXP = 8
REQ_G = 16
GROUPS = 16
TP = 8
PAGES_D = 12
ROWS = 8
ROW_TILES = PAGE // ROWS
TILES = PAGES_D + 1
ENTRIES = REQ_G * MAXP
GH = HEADS // KVH
BLOCKS = HD // REQ_G
SLOTS = GROUPS * REQ_G
SPAN = MAXP * PAGE
USUAL = 108
UNROLL = 16

VMEM = pl.BlockSpec(memory_space=pltpu.VMEM)
SMEM = pl.BlockSpec(memory_space=pltpu.SMEM)
HBM = pl.BlockSpec(memory_space=pltpu.HBM)
ANY = pl.BlockSpec(memory_space=pl.ANY)
LIMIT = 40 * 1024 * 1024


def cut_kernel(fresh_ref, owner_ref, length_ref, slot_ref, out_ref, pages, owners, facts, ints, sems, table_sem):
    copies = []
    for page in range(PAGES_D):
        copy = pltpu.make_async_copy(fresh_ref.at[page], pages.at[page], sems.at[page])
        copy.start()
        copies.append(copy)
    tables = [
        pltpu.make_async_copy(owner_ref, owners, table_sem.at[0]),
        pltpu.make_async_copy(length_ref, facts.at[0], table_sem.at[1]),
        pltpu.make_async_copy(slot_ref, facts.at[1], table_sem.at[2]),
    ]
    for copy in tables:
        copy.start()

    for page in range(PAGES_D):
        copies[page].wait()
        for rt in range(ROW_TILES):
            for half in range(2):
                for head in range(KVH):
                    row = (rt * 2 + half) * KVH + head
                    out_ref[row, page] = pages[page, head, rt, :, half * HD:(half + 1) * HD]

    for copy in tables:
        copy.wait()
    owner = owners[...]
    device = (owner * 43) >> 9
    place = device * TILES + (owner - device * PAGES_D)
    length = facts[0]
    ints[...] = jnp.zeros_like(ints)
    for block in range(BLOCKS):
        lanes = slice(block * REQ_G, (block + 1) * REQ_G)
        ints[:ROWS, lanes] = place
        ints[ROWS:ROWS + 1, lanes] = length & (PAGE - 1)
        ints[ROWS + 1:ROWS + 2, lanes] = length >> 6
        ints[ROWS + 2:ROWS + 3, lanes] = facts[1]
    block = lax.broadcasted_iota(jnp.int32, (ROWS, HD), 1) // REQ_G
    mine = lax.rem(lax.axis_index("group"), BLOCKS)
    tile = jnp.where(block == mine, ints[:ROWS], 0)
    tile = jnp.where(block == lax.rem(mine + 1, BLOCKS), ints[ROWS:], tile)
    tile = tile.astype(jnp.float32).astype(jnp.bfloat16)
    for row in range(GROUPS * TP):
        out_ref[row, PAGES_D] = tile


def cut(fresh, owner_table, lengths, decode_slot):
    return pl.pallas_call(
        cut_kernel,
        in_specs=[HBM, HBM, HBM, HBM],
        out_specs=VMEM,
        out_shape=pltpu.VMEM((GROUPS * TP, TILES, ROWS, HD), jnp.bfloat16),
        scratch_shapes=[
            pltpu.VMEM((PAGES_D, KVH, ROW_TILES, ROWS, 2 * HD), jnp.bfloat16),
            pltpu.VMEM((MAXP, REQ_G), jnp.int32),
            pltpu.VMEM((2, 1, REQ_G), jnp.int32),
            pltpu.VMEM((2 * ROWS, HD), jnp.int32),
            pltpu.SemaphoreType.DMA((PAGES_D,)),
            pltpu.SemaphoreType.DMA((3,)),
        ],
        compiler_params=pltpu.CompilerParams(vmem_limit_bytes=58000000),
        name="cut",
    )(
        fresh.reshape(PAGES_D, KVH, ROW_TILES, ROWS, 2 * HD),
        owner_table.T,
        lengths.reshape(1, REQ_G),
        decode_slot.reshape(1, REQ_G),
    )


def pick_kernel(cap, got_ref, out_ref, len_ref, over_ref, ints, table, sem):
    block = lax.broadcasted_iota(jnp.int32, (ROWS, HD), 1) // REQ_G
    which = lax.broadcasted_iota(jnp.int32, (SLOTS, HD), 0).astype(jnp.float32)
    sorted_rows = jnp.zeros((2 * ROWS, SLOTS), jnp.float32)
    for half in range(GROUPS // BLOCKS):
        place = jnp.zeros((ROWS, HD), jnp.float32)
        facts = jnp.zeros((ROWS, HD), jnp.float32)
        for k in range(BLOCKS):
            tile = got_ref[(half * BLOCKS + k) * TP * TILES + PAGES_D].astype(jnp.float32)
            place = jnp.where(block == k, tile, place)
            facts = jnp.where(block == (k + 1) % BLOCKS, tile, facts)
        facts = pltpu.roll(facts, HD - REQ_G, 1)
        home = (block + half * BLOCKS).astype(jnp.float32)
        rows = jnp.concatenate([place, facts[0:2], home[0:6]], axis=0).astype(jnp.bfloat16)
        here = jnp.where(facts[2:3] == which, 1.0, 0.0).astype(jnp.bfloat16)
        sorted_rows += lax.dot_general(
            rows, here, (((1,), (1,)), ((), ())), preferred_element_type=jnp.float32
        )
    sorted_rows = sorted_rows.astype(jnp.int32)
    length = sorted_rows[8:9] + sorted_rows[9:10] * PAGE
    count = (length + PAGE - 1) >> 6
    slot = lax.broadcasted_iota(jnp.int32, (ROWS, SLOTS), 1)
    first = jnp.broadcast_to(count, (ROWS, SLOTS))
    for step in (1, 2, 4, 8):
        first += jnp.where(slot % REQ_G >= step, pltpu.roll(first, step, 1), 0)
    over = jnp.where(first > cap, 1.0, 0.0)
    ints[:ROWS] = sorted_rows[:ROWS] + sorted_rows[10:11] * (TP * TILES)
    ints[ROWS:] = first - count + slot // REQ_G * cap
    copies = [
        pltpu.make_async_copy(ints.at[j], table.at[pl.ds(j * SLOTS, SLOTS)], sem.at[j])
        for j in range(MAXP + 1)
    ]
    for copy in copies:
        copy.start()
    len_ref[...] = length
    over_ref[0] = jnp.max(over).astype(jnp.int32)
    for copy in copies:
        copy.wait()

    def fill(group, clamp):
        for item in range(REQ_G):
            at = table[group * REQ_G + (ROWS * SLOTS + item)]
            span = out_ref.at[pl.ds(at, MAXP)]
            for j in reversed(range(MAXP)):
                tile = got_ref[table[group * REQ_G + (j * SLOTS + item)]]
                if clamp:
                    out_ref[jnp.minimum(at + j, GROUPS * cap - 1)] = tile
                else:
                    span[j] = tile

    def one_group(group, carry):
        fill(group, False)
        return carry

    lax.fori_loop(0, GROUPS - 1, one_group, 0)
    fill(GROUPS - 1, True)


def pick(got, cap):
    return pl.pallas_call(
        functools.partial(pick_kernel, cap),
        in_specs=[VMEM],
        out_specs=[VMEM, VMEM, SMEM],
        out_shape=[
            jax.ShapeDtypeStruct((GROUPS * cap, ROWS, HD), jnp.bfloat16),
            jax.ShapeDtypeStruct((1, SLOTS), jnp.int32),
            pltpu.SMEM((1,), jnp.int32),
        ],
        scratch_shapes=[
            pltpu.VMEM((2 * ROWS, SLOTS), jnp.int32),
            pltpu.SMEM(((MAXP + 1) * SLOTS,), jnp.int32),
            pltpu.SemaphoreType.DMA((MAXP + 1,)),
        ],
        compiler_params=pltpu.CompilerParams(vmem_limit_bytes=LIMIT),
        name="pick",
    )(got)


def serve_kernel(cap, len_ref, table_ref, arrived_ref, query_ref, new_ref, pool_ref, out_ref, tiles, sem):
    mine = lax.axis_index("group") * REQ_G

    def page_copy(slot, j):
        return pltpu.make_async_copy(
            tiles.at[slot * MAXP + j], pool_ref.at[table_ref[j, slot]], sem
        )

    row = lax.broadcasted_iota(jnp.int32, (ROWS, HD), 0)
    wide = lax.broadcasted_iota(jnp.int32, (ROWS, 2 * HD), 0)

    def fill(slot, first):
        length = len_ref[0, mine + slot]
        for j in range(MAXP):
            entry = jnp.minimum(first + j, cap - 1)
            for rt in range(ROW_TILES):
                old = row < length - (j * PAGE + rt * ROWS)
                for half in range(2):
                    x = arrived_ref[2 * rt + half, entry].astype(jnp.float32)
                    x = jnp.where(old, x, 0.0).astype(jnp.bfloat16)
                    tiles[slot * MAXP + j, rt, :, half * HD:(half + 1) * HD] = x
        late = new_ref[slot].astype(jnp.float32)
        for position in (length, length + STEPS - 1):
            j, rt = position // PAGE, position % PAGE // ROWS
            at = wide + (position // ROWS * ROWS - length)
            x = tiles[slot * MAXP + j, rt].astype(jnp.float32)
            for u in range(STEPS):
                x = jnp.where(at == u, late[u:u + 1], x)
            tiles[slot * MAXP + j, rt] = x.astype(jnp.bfloat16)
        for j in range(MAXP):
            page_copy(slot, j).start()
        return first + ((length + PAGE - 1) >> 6)

    lax.fori_loop(0, REQ_G, fill, jnp.int32(0))

    shape = (GH * STEPS, SPAN)
    step = lax.rem(lax.broadcasted_iota(jnp.int32, shape, 0), STEPS)
    ahead = lax.broadcasted_iota(jnp.int32, shape, 1) - step - 1

    def attend(first, carry):
        slots = [first * UNROLL + k for k in range(UNROLL)]
        scores = []
        for slot in slots:
            key = tiles[pl.ds(slot * MAXP, MAXP), :, :, :HD].reshape(SPAN, HD)
            products = lax.dot_general(
                query_ref[slot], key, (((1,), (1,)), ((), ())), preferred_element_type=jnp.float32
            )
            scores.append(jnp.where(ahead < len_ref[0, mine + slot], products * (HD ** -0.5), -jnp.inf))
        highest = [jnp.max(x, axis=1, keepdims=True) for x in scores]
        weights = [jnp.exp(x - y) for x, y in zip(scores, highest)]
        totals = [jnp.sum(x, axis=1, keepdims=True) for x in weights]
        probs = [(x / y).astype(jnp.bfloat16) for x, y in zip(weights, totals)]
        for slot, prob in zip(slots, probs):
            value = tiles[pl.ds(slot * MAXP, MAXP), :, :, HD:].reshape(SPAN, HD)
            mixed = jnp.dot(prob, value, preferred_element_type=jnp.float32).astype(jnp.bfloat16)
            for g in range(GH):
                out_ref[slot, :, g * HD:(g + 1) * HD] = mixed[g * STEPS:(g + 1) * STEPS]
        return carry

    lax.fori_loop(0, REQ_G // UNROLL, attend, 0)

    pltpu.make_async_copy(tiles, pool_ref, sem).wait()


def serve(lengths, table, arrived, queries, new_kv):
    return pl.pallas_call(
        functools.partial(serve_kernel, arrived.shape[1]),
        in_specs=[SMEM, SMEM, VMEM, VMEM, VMEM],
        out_specs=[ANY, VMEM],
        out_shape=[
            jax.ShapeDtypeStruct((ENTRIES, ROW_TILES, ROWS, 2 * HD), jnp.bfloat16),
            jax.ShapeDtypeStruct((REQ_G, STEPS, GH * HD), jnp.bfloat16),
        ],
        scratch_shapes=[
            pltpu.VMEM((ENTRIES, ROW_TILES, ROWS, 2 * HD), jnp.bfloat16),
            pltpu.SemaphoreType.DMA,
        ],
        compiler_params=pltpu.CompilerParams(vmem_limit_bytes=LIMIT),
        name="serve",
    )(lengths, table, arrived, queries, new_kv)


def shards(fresh, lengths, owner_table, decode_slot, decode_table, queries, new_kv):
    sent = cut(fresh, owner_table, lengths, decode_slot)
    got = lax.all_to_all(sent, ("group", "tp"), split_axis=0, concat_axis=0, tiled=True)
    got = got.reshape(GROUPS * TP * TILES, ROWS, HD)
    table = decode_table.T
    by_head = queries.reshape(REQ_G, STEPS, GH, HD).transpose(0, 2, 1, 3)
    by_head = by_head.reshape(REQ_G, GH * STEPS, HD)

    def deliver(packed, all_len, cap):
        arrived = lax.all_to_all(
            packed.reshape(GROUPS, cap, ROWS, HD), "group", split_axis=0, concat_axis=0, tiled=True
        )
        return serve(all_len, table, arrived, by_head, new_kv)

    def whole(packed, all_len):
        packed, all_len, _ = pick(got, ENTRIES)
        return deliver(packed, all_len, ENTRIES)

    packed, all_len, over = pick(got, USUAL)
    pool, attended = lax.switch(
        over[0], [lambda packed, all_len: deliver(packed, all_len, USUAL), whole], packed, all_len
    )
    return pool.reshape(ENTRIES, 1, PAGE, 2 * HD), attended


def solution(mesh):
    return jax.shard_map(
        shards,
        mesh=mesh,
        in_specs=(
            P(("group", "tp"), None, None, None),
            P("group"),
            P("group", None),
            P("group"),
            P("group", None),
            P("group", None, "tp"),
            P("group", None, "tp"),
        ),
        out_specs=(P("group", "tp", None, None), P("group", None, "tp")),
        check_vma=False,
    )
```
